32 devices in a mesh: dp: 16 (over z, x, core), tensor: 2 (over y).
Axes of the slice: x: 2, y: 2, z: 4, core: 2. Of those that a mesh axis runs over, the one named last changes fastest.
Arguments:
- hidden: bfloat16 [32, 1024, 1024], P('dp'), may hold values from -6 to 6
- segment_ids: int32 [32, 1024], P('dp'), may hold values from 0 to 3, never falling along the last dimension, each value on 1 to 800 neighbouring positions
- norm_gain: float32 [1024], replicated, may hold values from 0.1 to 1.9
- proj_gate: bfloat16 [1024, 2048], P(None, 'tensor'), may hold values from -0.1875 to 0.1875
- proj_value: bfloat16 [1024, 2048], P(None, 'tensor'), may hold values from -0.1875 to 0.1875
- proj_state: bfloat16 [1024, 256], replicated, may hold values from -0.1875 to 0.1875
- proj_step: bfloat16 [1024, 32], P(None, 'tensor'), may hold values from -0.1875 to 0.1875
- conv_value: float32 [4, 2048], P(None, 'tensor'), may hold values from -3 to 3
- conv_value_bias: float32 [2048], P('tensor'), may hold values from -3 to 3
- conv_state: float32 [4, 256], replicated, may hold values from -3 to 3
- conv_state_bias: float32 [256], replicated, may hold values from -3 to 3
- step_bias: float32 [32], P('tensor'), may hold values from -6 to -2
- decay_log: float32 [32], P('tensor'), may hold values from 0 to 2.77
- skip_gain: float32 [32], P('tensor'), may hold values from 0.5 to 1.5
- gate_gain: float32 [2048], P('tensor'), may hold values from 0.1 to 1.9
- proj_out: bfloat16 [1024, 2048], P(None, 'tensor'), may hold values from -0.125 to 0.125
- out_grad: bfloat16 [32, 1024, 1024], P('dp'), may hold values from -6 to 6
Outputs:
- block_out: bfloat16 [32, 1024, 1024], P('dp')
- grad_hidden: float32 [32, 1024, 1024], P('dp')
- grad_norm_gain: float32 [1024], replicated
- grad_proj_gate: float32 [1024, 2048], P('dp', 'tensor')
- grad_proj_value: float32 [1024, 2048], P('dp', 'tensor')
- grad_proj_state: float32 [1024, 256], P('dp')
- grad_proj_step: float32 [1024, 32], P('dp', 'tensor')
- grad_conv_value: float32 [4, 2048], P(None, 'tensor')
- grad_conv_value_bias: float32 [2048], P('tensor')
- grad_conv_state: float32 [4, 256], replicated
- grad_conv_state_bias: float32 [256], replicated
- grad_step_bias: float32 [32], P('tensor')
- grad_decay_log: float32 [32], P('tensor')
- grad_skip_gain: float32 [32], P('tensor')
- grad_gate_gain: float32 [2048], P('tensor')
- grad_proj_out: float32 [1024, 2048], P('dp', 'tensor')
The draws below stay inside these ranges and needn't reach their ends.
Inputs may be any that keep to these rules, and one draw needn't show every extreme that they name: `segment_ids`: tokens of a sequence with the same number form one document; numbers never fall along a sequence; each sequence holds 4 documents of 1 to 800 tokens, one of exactly 800.
All inputs are finite; a program needn't handle non-finite values.
Results may differ from the reference program's by a relative error of at most 0.019.
Values sent between devices are 32-bit elements; how exact they have to be, the bound alone decides.
A program may use at most 192 MiB of HBM per device.

```python
import math
import jax
import jax.numpy as jnp
import numpy as np
from jax import lax

D = 1024
HEADS = 32
HEAD_DIM = 64
STATE = 128
KERNEL = 4
LEN = 1024
DOCS = 4
INNER = 2048
MOST = 800
SEQUENCES = 32


def block_scale(key, shape, pieces, least, largest):
    loudness, own = 1.0, jax.random.fold_in(key, 6)
    for dim, blocks in pieces:
        steps = jnp.exp(jax.random.uniform(jax.random.fold_in(own, dim), (blocks,), jnp.float32, least / len(pieces), largest / len(pieces)))
        loudness = loudness * jnp.repeat(steps, shape[dim] // blocks).reshape([-1 if axis == dim else 1 for axis in range(len(shape))])
    return loudness


def length_profile(number_of, total, most, slope):
    portions = [(1 << 20) // math.isqrt(grade ** slope) + 1 for grade in range(2, number_of + 1)]
    surplus, holding = total - most - (number_of - 1), [1] * (number_of - 1)
    while surplus > 0:
        candidates = [i for i in range(number_of - 1) if holding[i] < most]
        pool, remaining = sum([portions[i] for i in candidates]), surplus
        for i in candidates:
            addition = min(most - holding[i], max(1, remaining * portions[i] // pool), surplus)
            holding[i] = holding[i] + addition
            surplus = surplus - addition
    return np.array([most] + holding)


def uneven(stream_key, number_of, total, reach, skew):
    if number_of == 2:
        one = jax.random.randint(stream_key, (), max(1, total - reach), min(reach, total - 1) + 1)
        return jnp.stack([one, total - one])
    tallies = jnp.asarray(length_profile(number_of, total, reach, skew), jnp.int32)
    couples = (number_of - 1) // 2
    giver, receiver = tallies[1:1 + 2 * couples:2], tallies[2:2 + 2 * couples:2]
    margin = jnp.minimum(giver - 1, reach - receiver)
    shifted = jax.random.randint(jax.random.fold_in(stream_key, 1), (couples,), 0, 1 << 20) % (margin + 1)
    tallies = tallies.at[1:1 + 2 * couples:2].set(giver - shifted).at[2:2 + 2 * couples:2].set(receiver + shifted)
    return tallies[jax.random.permutation(jax.random.fold_in(stream_key, 2), number_of)]


def noise(key, dims, scale, limit, cuts=(), kind=jnp.bfloat16):
    factor_of = block_scale(key, dims, cuts, -0.22, 0.18) if cuts else 1.0
    drawn = jax.random.normal(key, dims, jnp.float32) * scale * factor_of
    return jnp.minimum(jnp.maximum(drawn, -limit), limit).astype(kind)


def setup_inputs(seed: int = 0) -> dict:
    splits = jax.random.split(jax.random.key(seed), 18)
    hidden = noise(splits[0], (SEQUENCES, LEN, D), 1.0, 6.0, ((0, 16),))
    segment_ids = jax.vmap(lambda own: jnp.searchsorted(jnp.cumsum(uneven(own, DOCS, LEN, MOST, 0)), jnp.arange(LEN), side="right"))(jax.random.split(splits[1], SEQUENCES)).reshape((SEQUENCES, LEN)).astype(jnp.int32)
    norm_gain = jnp.clip(1.0 + 0.18 * jax.random.normal(splits[2], (D,), jnp.float32), 0.1, 1.9)
    proj_gate = noise(splits[3], (D, INNER), D ** -0.5, 0.1875, ((1, 2),))
    proj_value = noise(splits[4], (D, INNER), D ** -0.5, 0.1875, ((1, 2),))
    proj_state = noise(splits[5], (D, 2 * STATE), D ** -0.5, 0.1875)
    proj_step = noise(splits[6], (D, HEADS), D ** -0.5, 0.1875, ((1, 2),))
    conv_value = noise(splits[7], (KERNEL, INNER), KERNEL ** -0.5, 3.0, ((1, 2),), jnp.float32)
    conv_value_bias = noise(splits[8], (INNER,), 0.5, 3.0, ((0, 2),), jnp.float32)
    conv_state = noise(splits[9], (KERNEL, 2 * STATE), KERNEL ** -0.5, 3.0, (), jnp.float32)
    conv_state_bias = noise(splits[10], (2 * STATE,), 0.5, 3.0, (), jnp.float32)
    step_bias = jnp.clip(-6.0 + 4.0 * jax.random.uniform(splits[11], (HEADS,), jnp.float32) ** block_scale(splits[11], (HEADS,), ((0, 2),), -0.2, 0.2), -6.0, -2.0)
    decay_log = jnp.clip(2.77 * jax.random.uniform(splits[12], (HEADS,), jnp.float32) ** block_scale(splits[12], (HEADS,), ((0, 2),), -0.2, 0.2), 0.0, 2.77)
    skip_gain = jnp.clip(0.5 + 1.0 * jax.random.uniform(splits[13], (HEADS,), jnp.float32) ** block_scale(splits[13], (HEADS,), ((0, 2),), -0.2, 0.2), 0.5, 1.5)
    gate_gain = jnp.clip(1.0 + 0.18 * jax.random.normal(splits[14], (INNER,), jnp.float32), 0.1, 1.9)
    proj_out = noise(splits[15], (D, INNER), INNER ** -0.5, 0.125, ((1, 2),))
    out_grad = noise(splits[16], (SEQUENCES, LEN, D), 1.0, 6.0, ((0, 16),))
    return {"hidden": hidden, "segment_ids": segment_ids, "norm_gain": norm_gain, "proj_gate": proj_gate, "proj_value": proj_value, "proj_state": proj_state, "proj_step": proj_step, "conv_value": conv_value, "conv_value_bias": conv_value_bias, "conv_state": conv_state, "conv_state_bias": conv_state_bias, "step_bias": step_bias, "decay_log": decay_log, "skip_gain": skip_gain, "gate_gain": gate_gain, "proj_out": proj_out, "out_grad": out_grad}


epsilon = 1e-05
precise = lax.Precision.HIGHEST

@jax.custom_vjp
def low(v):
    return lax.optimization_barrier(v.astype(jnp.bfloat16)).astype(jnp.float32)

@jax.custom_vjp
def low_back(v):
    return v

def low_keep(v):
    return (low(v), None)

def low_pass(kept, grad):
    return (grad,)

def back_keep(v):
    return (v, None)

def back_low(kept, grad):
    return (low(grad),)
low.defvjp(low_keep, low_pass)
low_back.defvjp(back_keep, back_low)

def rounded_both(v):
    return low_back(low(v))

def lag_masks(segment_row):
    length = segment_row.shape[0]
    result = [jnp.ones((length,), jnp.float32)]
    for delay in range(1, KERNEL):
        earlier = jnp.concatenate([jnp.full((delay,), -1, jnp.int32), segment_row[:length - delay].astype(jnp.int32)])
        result.append((earlier == segment_row.astype(jnp.int32)).astype(jnp.float32))
    return result

def causal_conv(values, weight, conv_bias, doc_masks):
    length = values.shape[0]
    summed = conv_bias[None, :] + weight[KERNEL - 1][None, :] * values
    for delay in range(1, KERNEL):
        earlier = jnp.concatenate([jnp.zeros((delay, values.shape[1]), jnp.float32), values[:length - delay]], axis=0)
        summed = summed + weight[KERNEL - 1 - delay][None, :] * earlier * doc_masks[delay][:, None]
    return jax.nn.silu(summed)

def head_mix(values, states, step_raw, segment_row, step_bias, decay_log, skip_gain):
    length = values.shape[0]
    head_count = step_raw.shape[1]
    state_low = rounded_both(states)
    value_low = rounded_both(values)
    state_in = state_low[:, :STATE]
    state_out = state_low[:, STATE:]
    step_size = jax.nn.softplus(step_raw + step_bias[None, :])
    decay_rate = -jnp.exp(decay_log)
    running = jnp.cumsum(step_size * decay_rate[None, :], axis=0)
    places = jnp.arange(length)
    allowed = (places[:, None] >= places[None, :]) & (segment_row[:, None] == segment_row[None, :])
    affinity = jnp.dot(state_out, state_in.T, precision=precise)
    per_head = values.reshape(length, head_count, HEAD_DIM)
    low_head = value_low.reshape(length, head_count, HEAD_DIM)

    def one_head(items):
        run_col, step_col, head_values = items
        decays = jnp.exp(jnp.where(allowed, run_col[:, None] - run_col[None, :], -1e+30))
        mix_weights = rounded_both(decays * affinity * step_col[None, :])
        return jnp.dot(mix_weights, head_values, precision=precise)
    mixed_heads = lax.map(jax.checkpoint(one_head), (running.T, step_size.T, low_head.transpose(1, 0, 2)))
    mixed_out = mixed_heads.transpose(1, 0, 2) + skip_gain[None, :, None] * per_head
    return mixed_out.reshape(length, head_count * HEAD_DIM)

def residual_block(hidden_row, segment_row, norm_gain, proj_gate, proj_value, proj_state, proj_step, conv_value, conv_value_bias, conv_state, conv_state_bias, step_bias, decay_log, skip_gain, gate_gain, proj_out):
    row_scale = lax.rsqrt(lax.optimization_barrier(jnp.mean(hidden_row * hidden_row, axis=-1, keepdims=True)) + epsilon)
    normed = low(hidden_row * row_scale * norm_gain[None, :])
    gate_raw = low_back(jnp.dot(normed, proj_gate, precision=precise))
    value_raw = low_back(jnp.dot(normed, proj_value, precision=precise))
    state_raw = jnp.dot(normed, proj_state, precision=precise)
    step_raw = low_back(jnp.dot(normed, proj_step, precision=precise))
    doc_masks = lag_masks(segment_row)
    value_conv = causal_conv(value_raw, conv_value, conv_value_bias, doc_masks)
    state_conv = causal_conv(state_raw, conv_state, conv_state_bias, doc_masks)
    mixed_out = head_mix(value_conv, state_conv, step_raw, segment_row, step_bias, decay_log, skip_gain)
    gated = mixed_out * jax.nn.silu(gate_raw)
    gated_scale = lax.rsqrt(lax.optimization_barrier(jnp.mean(gated * gated, axis=-1, keepdims=True)) + epsilon)
    output_in = low(gated * gated_scale * gate_gain[None, :])
    return hidden_row + jnp.dot(output_in, proj_out.T, precision=precise)

def reference(hidden, segment_ids, norm_gain, proj_gate, proj_value, proj_state, proj_step, conv_value, conv_value_bias, conv_state, conv_state_bias, step_bias, decay_log, skip_gain, gate_gain, proj_out, out_grad):
    weights = tuple((w.astype(jnp.float32) for w in (norm_gain, proj_gate, proj_value, proj_state, proj_step, conv_value, conv_value_bias, conv_state, conv_state_bias, step_bias, decay_log, skip_gain, gate_gain, proj_out)))

    def per_sequence(totals, items):
        hidden_row, segment_row, cotangent = items

        def forward(inputs, *params):
            return residual_block(inputs, segment_row, *params)
        result, pullback = jax.vjp(forward, hidden_row.astype(jnp.float32), *weights)
        grads = pullback(cotangent.astype(jnp.float32))
        totals = tuple((t + g for t, g in zip(totals, grads[1:])))
        return (totals, (result.astype(jnp.bfloat16), grads[0]))
    zeros = tuple((jnp.zeros_like(w) for w in weights))
    totals, (block_out, grad_hidden) = lax.scan(per_sequence, zeros, (hidden, segment_ids, out_grad))
    g_norm, g_gate, g_value, g_state, g_step, g_conv_value, g_conv_value_bias, g_conv_state, g_conv_state_bias, g_step_bias, g_decay, g_skip, g_gate_gain, g_out = totals
    return (block_out, grad_hidden, g_norm, g_gate, g_value, g_state, g_step, g_conv_value, g_conv_value_bias, g_conv_state, g_conv_state_bias, g_step_bias, g_decay, g_skip, g_gate_gain, g_out)
```

```python
import functools

import jax
import jax.numpy as jnp
from jax import lax
from jax.sharding import PartitionSpec as P

HEAD_DIM = 64
STATE = 128
KERNEL = 4


epsilon = 1e-05
precise = lax.Precision.HIGHEST


def lag_masks(segment_row):
    length = segment_row.shape[0]
    result = [jnp.ones((length,), jnp.float32)]
    for delay in range(1, KERNEL):
        earlier = jnp.concatenate(
            [jnp.full((delay,), -1, jnp.int32), segment_row[: length - delay]]
        )
        result.append((earlier == segment_row).astype(jnp.float32))
    return result


def causal_conv(values, weight, conv_bias, doc_masks):
    length = values.shape[0]
    summed = conv_bias[None, :] + weight[KERNEL - 1][None, :] * values
    for delay in range(1, KERNEL):
        earlier = jnp.concatenate(
            [jnp.zeros((delay, values.shape[1]), jnp.float32), values[: length - delay]], axis=0
        )
        summed = summed + weight[KERNEL - 1 - delay][None, :] * earlier * doc_masks[delay][:, None]
    return jax.nn.silu(summed)


CHUNK = 128


def head_mix(values, states, step_raw, segment_row, step_bias, decay_log, skip_gain):
    length, inner = values.shape
    heads = step_raw.shape[1]
    chunks = length // CHUNK
    step_size = jax.nn.softplus(step_raw + step_bias[None, :])
    decay_rate = -jnp.exp(decay_log)
    places = jnp.arange(CHUNK)
    lower = places[:, None] >= places[None, :]
    drop = (step_size * decay_rate[None, :]).reshape(chunks, CHUNK, heads)
    running = jnp.einsum("ts,csh->cth", lower.astype(jnp.float32), drop, precision=precise)
    segments = segment_row.reshape(chunks, CHUNK)
    last = segments[:, -1]
    before = jnp.concatenate([jnp.full((1,), -1, jnp.int32), last[:-1]])
    allowed = lower[None] & (segments[:, :, None] == segments[:, None, :])
    state_in = states[:, :STATE].astype(jnp.bfloat16).reshape(chunks, CHUNK, STATE)
    state_out = states[:, STATE:].astype(jnp.bfloat16).reshape(chunks, CHUNK, STATE)
    affinity = jnp.einsum("ctn,csn->cts", state_out, state_in, preferred_element_type=jnp.float32)
    running_head = running.transpose(0, 2, 1)
    step_head = step_size.reshape(chunks, CHUNK, heads).transpose(0, 2, 1)
    decays = jnp.exp(
        jnp.where(
            allowed[:, None], running_head[:, :, :, None] - running_head[:, :, None, :], -1e30
        )
    )
    mixing = (decays * affinity[:, None] * step_head[:, :, None, :]).astype(jnp.bfloat16)
    low_head = values.astype(jnp.bfloat16).reshape(chunks, CHUNK, heads, HEAD_DIM)
    near = jnp.einsum("chts,cshp->cthp", mixing, low_head, preferred_element_type=jnp.float32)
    near = near.reshape(chunks, CHUNK, inner)

    spread = (jnp.arange(inner)[None, :] // HEAD_DIM == jnp.arange(heads)[:, None]).astype(
        jnp.float32
    )
    total = running[:, -1, :]
    at_end = (segments == last[:, None]).astype(jnp.float32)
    from_start = (segments == before[:, None]).astype(jnp.float32)
    keep_scale = (
        jnp.exp(total[:, None, :] - running)
        * step_size.reshape(chunks, CHUNK, heads)
        * at_end[:, :, None]
    )
    read_scale = jnp.exp(running) * from_start[:, :, None]
    carry = jnp.exp(total) * (last == before).astype(jnp.float32)[:, None]
    keep_wide = jnp.einsum("cth,hi->cti", keep_scale, spread, precision=lax.Precision.HIGH)
    read_wide = jnp.einsum("cth,hi->cti", read_scale, spread, precision=lax.Precision.HIGH)
    carry_wide = jnp.einsum("ch,hi->ci", carry, spread, precision=precise)
    kept = (values.reshape(chunks, CHUNK, inner) * keep_wide).astype(jnp.bfloat16)
    gained = jnp.einsum("csn,csi->cni", state_in, kept, preferred_element_type=jnp.float32)
    held = jnp.zeros((STATE, inner), jnp.float32)
    entry = []
    for c in range(chunks):
        entry.append(held.astype(jnp.bfloat16))
        held = held * carry_wide[c][None, :] + gained[c]
    entry = jnp.stack(entry)
    far = jnp.einsum("ctn,cni->cti", state_out, entry, preferred_element_type=jnp.float32)
    mixed = (near + far * read_wide).reshape(length, inner)
    return mixed + jnp.repeat(skip_gain, HEAD_DIM)[None, :] * values


def mixer(
    segment_row,
    value_row,
    state_row,
    step_row,
    conv_value,
    conv_value_bias,
    conv_state,
    conv_state_bias,
    step_bias,
    decay_log,
    skip_gain,
):
    doc_masks = lag_masks(segment_row)
    value_conv = causal_conv(value_row, conv_value, conv_value_bias, doc_masks)
    state_conv = causal_conv(state_row, conv_state, conv_state_bias, doc_masks)
    return head_mix(value_conv, state_conv, step_row, segment_row, step_bias, decay_log, skip_gain)


def right_product(left, weight):
    return lax.dot_general(
        left, weight, (((1,), (1,)), ((), ())), preferred_element_type=jnp.float32
    )


def token_product(left, right):
    return lax.dot_general(
        left, right, (((0,), (0,)), ((), ())), preferred_element_type=jnp.float32
    )


def tensor_sum(part):
    count = lax.axis_size("tensor")
    if count == 1:
        return part
    if count == 2:
        return part + lax.ppermute(part, "tensor", [(0, 1), (1, 0)])
    return lax.psum(part, "tensor")


def local(
    hidden,
    segment_ids,
    norm_gain,
    proj_gate,
    proj_value,
    proj_state,
    proj_step,
    conv_value,
    conv_value_bias,
    conv_state,
    conv_state_bias,
    step_bias,
    decay_log,
    skip_gain,
    gate_gain,
    proj_out,
    out_grad,
):
    seq_count, length, width = hidden.shape
    local_inner = proj_gate.shape[1]
    local_heads = proj_step.shape[1]
    state_width = proj_state.shape[1]
    tensor_count = lax.axis_size("tensor")
    inner_total = local_inner * tensor_count
    every = range(seq_count)

    wides = [hidden[s].astype(jnp.float32) for s in every]
    row_scales = [
        lax.rsqrt(jnp.mean(w * w, axis=-1, keepdims=True) + epsilon) for w in wides
    ]
    normeds = [
        (w * r * norm_gain[None, :]).astype(jnp.bfloat16) for w, r in zip(wides, row_scales)
    ]
    params = (
        conv_value,
        conv_value_bias,
        conv_state,
        conv_state_bias,
        step_bias,
        decay_log,
        skip_gain,
    )
    gate_raws, mixed_outs, mixer_backs, gateds, squares = [], [], [], [], []
    for s in every:
        gate_raw = jnp.dot(normeds[s], proj_gate, preferred_element_type=jnp.float32)
        value_raw = jnp.dot(normeds[s], proj_value, preferred_element_type=jnp.float32)
        state_raw = jnp.dot(normeds[s], proj_state, preferred_element_type=jnp.float32)
        step_raw = jnp.dot(normeds[s], proj_step, preferred_element_type=jnp.float32)
        mixed_out, back = jax.vjp(
            jax.checkpoint(functools.partial(mixer, segment_ids[s])),
            value_raw,
            state_raw,
            step_raw,
            *params,
        )
        gated = mixed_out * jax.nn.silu(gate_raw)
        gate_raws.append(gate_raw)
        mixed_outs.append(mixed_out)
        mixer_backs.append(back)
        gateds.append(gated)
        squares.append(jnp.sum(gated * gated, axis=-1))

    d_output_ins = [
        jnp.dot(out_grad[s], proj_out, preferred_element_type=jnp.float32) for s in every
    ]
    inners = [
        jnp.sum(d_output_ins[s] * gate_gain[None, :] * gateds[s], axis=-1) for s in every
    ]
    both = lax.psum(jnp.stack(squares + inners), "tensor")
    block_outs, output_ins, d_gates, d_mixeds = [], [], [], []
    grad_gate_gain = jnp.zeros((local_inner,), jnp.float32)
    for s in every:
        gated, gate_raw = gateds[s], gate_raws[s]
        gated_scale = lax.rsqrt(both[s] / inner_total + epsilon)[:, None]
        gate_inner = both[seq_count + s][:, None]
        output_in = (gated * gated_scale * gate_gain[None, :]).astype(jnp.bfloat16)
        branch = tensor_sum(right_product(output_in, proj_out))
        block_outs.append((wides[s] + branch).astype(jnp.bfloat16))
        d_output_in = d_output_ins[s]
        grad_gate_gain = grad_gate_gain + jnp.sum(d_output_in * gated * gated_scale, axis=0)
        weighted = d_output_in * gate_gain[None, :]
        d_gated = gated_scale * weighted - gated_scale**3 * gated * gate_inner / inner_total
        sigma = jax.nn.sigmoid(gate_raw)
        d_mixeds.append(d_gated * gate_raw * sigma)
        d_gates.append(
            (d_gated * mixed_outs[s] * sigma * (1.0 + gate_raw * (1.0 - sigma))).astype(
                jnp.bfloat16
            )
        )
        output_ins.append(output_in)

    normed_all = jnp.concatenate(normeds, axis=0)
    early = lax.psum_scatter(
        jnp.concatenate(
            [
                token_product(normed_all, jnp.concatenate(d_gates, axis=0)),
                token_product(
                    out_grad.reshape(seq_count * length, width),
                    jnp.concatenate(output_ins, axis=0),
                ),
            ],
            axis=1,
        ),
        "dp",
        scatter_dimension=0,
        tiled=True,
    )

    late_weight = jnp.concatenate([proj_value, proj_state, proj_step], axis=1)
    param_grads, lates, grad_hiddens = None, [], []
    grad_norm_gain = jnp.zeros((width,), jnp.float32)
    for s in every:
        d_value, d_state, d_step, *grads = mixer_backs[s](d_mixeds[s])
        param_grads = grads if s == 0 else [a + b for a, b in zip(param_grads, grads)]
        late = jnp.concatenate([d_value, d_state, d_step], axis=1).astype(jnp.bfloat16)
        lates.append(late)
        part = right_product(d_gates[s], proj_gate) + right_product(late, late_weight)
        row_scale, wide = row_scales[s], wides[s]
        grad_norm_gain = grad_norm_gain + jnp.sum(part * wide * row_scale, axis=0)
        d_scaled = tensor_sum(part) * norm_gain[None, :]
        norm_inner = jnp.sum(d_scaled * wide, axis=-1, keepdims=True)
        grad_hiddens.append(
            out_grad[s].astype(jnp.float32)
            + row_scale * d_scaled
            - row_scale**3 * wide * norm_inner / width
        )
    later = lax.psum_scatter(
        token_product(normed_all, jnp.concatenate(lates, axis=0)),
        "dp",
        scatter_dimension=0,
        tiled=True,
    )
    edge_state = local_inner + state_width
    grad_proj_state = lax.psum(later[:, local_inner:edge_state], "tensor")

    g_cv, g_cvb, g_cs, g_csb, g_sb, g_dl, g_sg = param_grads
    own = [g_cv, g_cvb, g_sb, g_dl, g_sg, grad_gate_gain]
    shared = [g_cs, g_csb, grad_norm_gain]
    own_flat = jnp.concatenate([g.reshape(-1) for g in own])
    place = lax.axis_index("tensor")
    mine = (jnp.arange(tensor_count) == place)[:, None]
    slots = jnp.where(mine, own_flat[None, :], 0.0).reshape(-1)
    packed = lax.psum(
        jnp.concatenate([slots] + [g.reshape(-1) for g in shared]), ("dp", "tensor")
    )
    own_sum = lax.dynamic_slice(packed, (place * own_flat.shape[0],), (own_flat.shape[0],))
    shared_sum = packed[slots.shape[0] :]

    def split(flat, like):
        result, edge = [], 0
        for g in like:
            result.append(flat[edge : edge + g.size].reshape(g.shape))
            edge += g.size
        return result

    r_cv, r_cvb, r_sb, r_dl, r_sg, r_gg = split(own_sum, own)
    r_cs, r_csb, r_ng = split(shared_sum, shared)
    return (
        jnp.stack(block_outs),
        jnp.stack(grad_hiddens),
        r_ng,
        early[:, :local_inner],
        later[:, :local_inner],
        grad_proj_state,
        later[:, edge_state:],
        r_cv,
        r_cvb,
        r_cs,
        r_csb,
        r_sb,
        r_dl,
        r_sg,
        r_gg,
        early[:, local_inner:],
    )


def solution(mesh):
    in_specs = (
        P("dp", None, None),
        P("dp", None),
        P(),
        P(None, "tensor"),
        P(None, "tensor"),
        P(),
        P(None, "tensor"),
        P(None, "tensor"),
        P("tensor"),
        P(),
        P(),
        P("tensor"),
        P("tensor"),
        P("tensor"),
        P("tensor"),
        P(None, "tensor"),
        P("dp", None, None),
    )
    out_specs = (
        P("dp", None, None),
        P("dp", None, None),
        P(),
        P("dp", "tensor"),
        P("dp", "tensor"),
        P("dp", None),
        P("dp", "tensor"),
        P(None, "tensor"),
        P("tensor"),
        P(),
        P(),
        P("tensor"),
        P("tensor"),
        P("tensor"),
        P("tensor"),
        P("dp", "tensor"),
    )
    return jax.shard_map(local, mesh=mesh, in_specs=in_specs, out_specs=out_specs, check_vma=False)
```

```python
import functools

import jax
import jax.numpy as jnp
from jax import lax
from jax.sharding import PartitionSpec as P

HEAD_DIM = 64
STATE = 128
KERNEL = 4


epsilon = 1e-05
precise = lax.Precision.HIGHEST


def lag_masks(segment_row):
    length = segment_row.shape[0]
    result = [jnp.ones((length,), jnp.float32)]
    for delay in range(1, KERNEL):
        earlier = jnp.concatenate(
            [jnp.full((delay,), -1, jnp.int32), segment_row[: length - delay]]
        )
        result.append((earlier == segment_row).astype(jnp.float32))
    return result


def causal_conv(values, weight, conv_bias, doc_masks):
    length = values.shape[0]
    summed = conv_bias[None, :] + weight[KERNEL - 1][None, :] * values
    for delay in range(1, KERNEL):
        earlier = jnp.concatenate(
            [jnp.zeros((delay, values.shape[1]), jnp.float32), values[: length - delay]], axis=0
        )
        summed = summed + weight[KERNEL - 1 - delay][None, :] * earlier * doc_masks[delay][:, None]
    return jax.nn.silu(summed)


CHUNK = 128


def head_mix(values, states, step_raw, segment_row, step_bias, decay_log, skip_gain):
    length, inner = values.shape
    heads = step_raw.shape[1]
    chunks = length // CHUNK
    step_size = jax.nn.softplus(step_raw + step_bias[None, :])
    decay_rate = -jnp.exp(decay_log)
    places = jnp.arange(CHUNK)
    lower = places[:, None] >= places[None, :]
    drop = (step_size * decay_rate[None, :]).reshape(chunks, CHUNK, heads)
    running = jnp.einsum("ts,csh->cth", lower.astype(jnp.float32), drop, precision=precise)
    segments = segment_row.reshape(chunks, CHUNK)
    last = segments[:, -1]
    before = jnp.concatenate([jnp.full((1,), -1, jnp.int32), last[:-1]])
    allowed = lower[None] & (segments[:, :, None] == segments[:, None, :])
    state_in = states[:, :STATE].astype(jnp.bfloat16).reshape(chunks, CHUNK, STATE)
    state_out = states[:, STATE:].astype(jnp.bfloat16).reshape(chunks, CHUNK, STATE)
    affinity = jnp.einsum("ctn,csn->cts", state_out, state_in, preferred_element_type=jnp.float32)
    running_head = running.transpose(0, 2, 1)
    step_head = step_size.reshape(chunks, CHUNK, heads).transpose(0, 2, 1)
    decays = jnp.exp(
        jnp.where(
            allowed[:, None], running_head[:, :, :, None] - running_head[:, :, None, :], -1e30
        )
    )
    mixing = (decays * affinity[:, None] * step_head[:, :, None, :]).astype(jnp.bfloat16)
    low_head = values.astype(jnp.bfloat16).reshape(chunks, CHUNK, heads, HEAD_DIM)
    near = jnp.einsum("chts,cshp->cthp", mixing, low_head, preferred_element_type=jnp.float32)
    near = near.reshape(chunks, CHUNK, inner)

    spread = (jnp.arange(inner)[None, :] // HEAD_DIM == jnp.arange(heads)[:, None]).astype(
        jnp.float32
    )
    total = running[:, -1, :]
    at_end = (segments == last[:, None]).astype(jnp.float32)
    from_start = (segments == before[:, None]).astype(jnp.float32)
    keep_scale = (
        jnp.exp(total[:, None, :] - running)
        * step_size.reshape(chunks, CHUNK, heads)
        * at_end[:, :, None]
    )
    read_scale = jnp.exp(running) * from_start[:, :, None]
    carry = jnp.exp(total) * (last == before).astype(jnp.float32)[:, None]
    keep_wide = jnp.einsum("cth,hi->cti", keep_scale, spread, precision=lax.Precision.HIGH)
    read_wide = jnp.einsum("cth,hi->cti", read_scale, spread, precision=lax.Precision.HIGH)
    carry_wide = jnp.einsum("ch,hi->ci", carry, spread, precision=precise)
    kept = (values.reshape(chunks, CHUNK, inner) * keep_wide).astype(jnp.bfloat16)
    gained = jnp.einsum("csn,csi->cni", state_in, kept, preferred_element_type=jnp.float32)
    held = jnp.zeros((STATE, inner), jnp.float32)
    entry = []
    for c in range(chunks):
        entry.append(held.astype(jnp.bfloat16))
        held = held * carry_wide[c][None, :] + gained[c]
    entry = jnp.stack(entry)
    far = jnp.einsum("ctn,cni->cti", state_out, entry, preferred_element_type=jnp.float32)
    mixed = (near + far * read_wide).reshape(length, inner)
    return mixed + jnp.repeat(skip_gain, HEAD_DIM)[None, :] * values


def mixer(
    segment_row,
    value_row,
    state_row,
    step_row,
    conv_value,
    conv_value_bias,
    conv_state,
    conv_state_bias,
    step_bias,
    decay_log,
    skip_gain,
):
    doc_masks = lag_masks(segment_row)
    value_conv = causal_conv(value_row, conv_value, conv_value_bias, doc_masks)
    state_conv = causal_conv(state_row, conv_state, conv_state_bias, doc_masks)
    return head_mix(value_conv, state_conv, step_row, segment_row, step_bias, decay_log, skip_gain)


def right_product(left, weight):
    return lax.dot_general(
        left, weight, (((1,), (1,)), ((), ())), preferred_element_type=jnp.float32
    )


def token_product(left, right):
    return lax.dot_general(
        left, right, (((0,), (0,)), ((), ())), preferred_element_type=jnp.float32
    )


def tensor_others(part):
    count = lax.axis_size("tensor")
    if count == 2:
        return lax.ppermute(part, "tensor", [(0, 1), (1, 0)])
    return lax.psum(part, "tensor")


def tensor_join(part, others):
    return part + others if lax.axis_size("tensor") == 2 else others


def after(value, *earlier):
    return lax.optimization_barrier((value, *earlier))[0]


def local(
    hidden,
    segment_ids,
    norm_gain,
    proj_gate,
    proj_value,
    proj_state,
    proj_step,
    conv_value,
    conv_value_bias,
    conv_state,
    conv_state_bias,
    step_bias,
    decay_log,
    skip_gain,
    gate_gain,
    proj_out,
    out_grad,
):
    seq_count, length, width = hidden.shape
    local_inner = proj_gate.shape[1]
    local_heads = proj_step.shape[1]
    state_width = proj_state.shape[1]
    tensor_count = lax.axis_size("tensor")
    inner_total = local_inner * tensor_count
    every = range(seq_count)

    wides = [hidden[s].astype(jnp.float32) for s in every]
    row_scales = [
        lax.rsqrt(jnp.mean(w * w, axis=-1, keepdims=True) + epsilon) for w in wides
    ]
    normeds = [
        (w * r * norm_gain[None, :]).astype(jnp.bfloat16) for w, r in zip(wides, row_scales)
    ]
    params = (
        conv_value,
        conv_value_bias,
        conv_state,
        conv_state_bias,
        step_bias,
        decay_log,
        skip_gain,
    )
    gate_raws, mixed_outs, mixer_backs, gateds, squares = [], [], [], [], []
    for s in every:
        gate_raw = jnp.dot(normeds[s], proj_gate, preferred_element_type=jnp.float32)
        value_raw = jnp.dot(normeds[s], proj_value, preferred_element_type=jnp.float32)
        state_raw = jnp.dot(normeds[s], proj_state, preferred_element_type=jnp.float32)
        step_raw = jnp.dot(normeds[s], proj_step, preferred_element_type=jnp.float32)
        mixed_out, back = jax.vjp(
            jax.checkpoint(functools.partial(mixer, segment_ids[s])),
            value_raw,
            state_raw,
            step_raw,
            *params,
        )
        gated = mixed_out * jax.nn.silu(gate_raw)
        gate_raws.append(gate_raw)
        mixed_outs.append(mixed_out)
        mixer_backs.append(back)
        gateds.append(gated)
        squares.append(jnp.sum(gated * gated, axis=-1))

    d_output_ins = [
        jnp.dot(out_grad[s], proj_out, preferred_element_type=jnp.float32) for s in every
    ]
    inners = [
        jnp.sum(d_output_ins[s] * gate_gain[None, :] * gateds[s], axis=-1) for s in every
    ]
    both = lax.psum(jnp.stack(squares + inners), "tensor")
    branches, received, output_ins, d_gates, d_mixeds = [], [], [], [], []
    grad_gate_gain = jnp.zeros((local_inner,), jnp.float32)
    for s in every:
        gated, gate_raw = gateds[s], gate_raws[s]
        gated_scale = lax.rsqrt(both[s] / inner_total + epsilon)[:, None]
        gate_inner = both[seq_count + s][:, None]
        output_in = (gated * gated_scale * gate_gain[None, :]).astype(jnp.bfloat16)
        branches.append(right_product(output_in, proj_out))
        received.append(tensor_others(branches[s]))
        d_output_in = d_output_ins[s]
        grad_gate_gain = grad_gate_gain + jnp.sum(d_output_in * gated * gated_scale, axis=0)
        weighted = d_output_in * gate_gain[None, :]
        d_gated = gated_scale * weighted - gated_scale**3 * gated * gate_inner / inner_total
        sigma = jax.nn.sigmoid(gate_raw)
        d_mixeds.append(d_gated * gate_raw * sigma)
        d_gates.append(
            (d_gated * mixed_outs[s] * sigma * (1.0 + gate_raw * (1.0 - sigma))).astype(
                jnp.bfloat16
            )
        )
        output_ins.append(output_in)

    normed_all = jnp.concatenate(normeds, axis=0)
    early_part = jnp.concatenate(
        [
            token_product(normed_all, jnp.concatenate(d_gates, axis=0)),
            token_product(
                out_grad.reshape(seq_count * length, width),
                jnp.concatenate(output_ins, axis=0),
            ),
        ],
        axis=1,
    )
    early = lax.psum_scatter(early_part, "dp", scatter_dimension=0, tiled=True)

    late_weight = jnp.concatenate([proj_value, proj_state, proj_step], axis=1)
    param_grads, lates, parts, others, grad_hiddens = None, [], [], [], []
    waits = (early_part, *branches)
    grad_norm_gain = jnp.zeros((width,), jnp.float32)
    for s in every:
        d_value, d_state, d_step, *grads = mixer_backs[s](after(d_mixeds[s], *waits))
        param_grads = grads if s == 0 else [a + b for a, b in zip(param_grads, grads)]
        late = jnp.concatenate([d_value, d_state, d_step], axis=1).astype(jnp.bfloat16)
        lates.append(late)
        part = right_product(d_gates[s], proj_gate) + right_product(late, late_weight)
        grad_norm_gain = grad_norm_gain + jnp.sum(part * wides[s] * row_scales[s], axis=0)
        parts.append(part)
        if s < seq_count - 1:
            parts[s] = after(part, received[s])
            others.append(tensor_others(parts[s]))
            waits = (part, received[s])
    edge_state = local_inner + state_width
    g_cv, g_cvb, g_cs, g_csb, g_sb, g_dl, g_sg = param_grads
    own = [g_cv, g_cvb, g_sb, g_dl, g_sg, grad_gate_gain]
    shared = [g_cs, g_csb, grad_norm_gain]
    own_flat = jnp.concatenate([g.reshape(-1) for g in own])
    place = lax.axis_index("tensor")
    mine = (jnp.arange(tensor_count) == place)[:, None]
    slots = jnp.where(mine, own_flat[None, :], 0.0).reshape(-1)
    packed = lax.psum(
        after(
            jnp.concatenate([slots] + [g.reshape(-1) for g in shared]),
            early,
            received[-1],
            *others,
        ),
        ("dp", "tensor"),
    )
    own_sum = lax.dynamic_slice(packed, (place * own_flat.shape[0],), (own_flat.shape[0],))
    shared_sum = packed[slots.shape[0] :]

    later = lax.psum_scatter(
        token_product(normed_all, after(jnp.concatenate(lates, axis=0), packed)),
        "dp",
        scatter_dimension=0,
        tiled=True,
    )
    block_outs = []
    for s in every:
        if s == seq_count - 1:
            parts[s] = after(parts[s], packed)
            others.append(tensor_others(parts[s]))
        d_scaled = tensor_join(parts[s], others[s]) * norm_gain[None, :]
        row_scale, wide = row_scales[s], wides[s]
        norm_inner = jnp.sum(d_scaled * wide, axis=-1, keepdims=True)
        grad_hiddens.append(
            out_grad[s].astype(jnp.float32)
            + row_scale * d_scaled
            - row_scale**3 * wide * norm_inner / width
        )
        branch = tensor_join(branches[s], received[s])
        block_outs.append((wide + branch).astype(jnp.bfloat16))
    grad_proj_state = lax.psum(later[:, local_inner:edge_state], "tensor")

    def split(flat, like):
        result, edge = [], 0
        for g in like:
            result.append(flat[edge : edge + g.size].reshape(g.shape))
            edge += g.size
        return result

    r_cv, r_cvb, r_sb, r_dl, r_sg, r_gg = split(own_sum, own)
    r_cs, r_csb, r_ng = split(shared_sum, shared)
    return (
        jnp.stack(block_outs),
        jnp.stack(grad_hiddens),
        r_ng,
        early[:, :local_inner],
        later[:, :local_inner],
        grad_proj_state,
        later[:, edge_state:],
        r_cv,
        r_cvb,
        r_cs,
        r_csb,
        r_sb,
        r_dl,
        r_sg,
        r_gg,
        early[:, local_inner:],
    )


def solution(mesh):
    in_specs = (
        P("dp", None, None),
        P("dp", None),
        P(),
        P(None, "tensor"),
        P(None, "tensor"),
        P(),
        P(None, "tensor"),
        P(None, "tensor"),
        P("tensor"),
        P(),
        P(),
        P("tensor"),
        P("tensor"),
        P("tensor"),
        P("tensor"),
        P(None, "tensor"),
        P("dp", None, None),
    )
    out_specs = (
        P("dp", None, None),
        P("dp", None, None),
        P(),
        P("dp", "tensor"),
        P("dp", "tensor"),
        P("dp", None),
        P("dp", "tensor"),
        P(None, "tensor"),
        P("tensor"),
        P(),
        P(),
        P("tensor"),
        P("tensor"),
        P("tensor"),
        P("tensor"),
        P("dp", "tensor"),
    )
    return jax.shard_map(local, mesh=mesh, in_specs=in_specs, out_specs=out_specs, check_vma=False)
```
